256 devices in a mesh: ta: 4 (over y), ha: 4 (over x), wa: 16 (over z, core).
Axes of the slice: x: 4, y: 4, z: 8, core: 2. Of those that a mesh axis runs over, the one named last changes fastest.
Arguments:
- video: bfloat16 [64, 32, 80, 384], P('ta', 'ha', 'wa'), may hold values from -6 to 6
- gain_first: float32 [384], replicated, may hold values from 0.1 to 1.9
- conv_first: bfloat16 [27, 384, 384], P(None, None, 'wa'), may hold values from -0.0625 to 0.0625
- gain_second: float32 [384], replicated, may hold values from 0.1 to 1.9
- conv_second: bfloat16 [27, 384, 384], P(None, None, 'wa'), may hold values from -0.0625 to 0.0625
- gain_attn: float32 [384], replicated, may hold values from 0.1 to 1.9
- w_qkv: bfloat16 [384, 1152], replicated, may hold values from -0.35721725 to 0.35721725
- w_proj: bfloat16 [384, 384], replicated, may hold values from -0.3125 to 0.3125
Outputs:
- decoded: bfloat16 [64, 32, 80, 384], P(('ta', 'wa'), 'ha')
The draws below stay inside these ranges and needn't reach their ends.
All inputs are finite; a program needn't handle non-finite values.
Results may differ from the reference program's by a relative error of at most 0.013.
Values may be sent and summed in bfloat16 or wider, within the bound.
No kernel may reach another device: no remote copies, remote signals or barrier semaphores. Data moves between devices by JAX's collectives and lax.ppermute only.
A program may use at most 320 MiB of HBM per device.

```python
import jax
import jax.numpy as jnp
from jax import lax

D = 384
FRAMES = 64
HEIGHT = 32
WIDTH = 80


def draw_w_qkv(key, part):
    key = jax.random.fold_in(key, 11)
    base = jnp.clip(jax.random.normal(key, (D, 3 * D), jnp.float32), -3.4, 3.4) * D ** (-0.5)
    return jnp.concatenate([2.0 * base[:, :2 * D], base[:, 2 * D:]], axis=1).astype(jnp.bfloat16)


def levels(key, shape, shards, least, top_value):
    loudness, own = 1.0, jax.random.fold_in(key, 6)
    for dim, blocks in shards:
        steps = jnp.exp(jax.random.uniform(jax.random.fold_in(own, dim), (blocks,), jnp.float32, least / len(shards), top_value / len(shards)))
        loudness = loudness * jnp.repeat(steps, shape[dim] // blocks).reshape([-1 if axis == dim else 1 for axis in range(len(shape))])
    return loudness


def noise(own_key, extent, width, most, pieces=(), kind=jnp.bfloat16):
    values = jax.random.normal(own_key, extent, jnp.float32) * width
    if len(pieces) > 0:
        values = levels(own_key, extent, pieces, -0.22, 0.18) * values
    return jnp.clip(values, min=-most, max=most).astype(kind)


def setup_inputs(seed: int = 0) -> dict:
    arg_keys = jax.random.split(jax.random.key(seed), 9)
    return {
        "video": noise(arg_keys[0], (FRAMES, HEIGHT, WIDTH, D), 1.0, 6.0, ((0, 4), (1, 4), (2, 16))),
        "gain_first": jnp.clip(1.0 + 0.18 * jax.random.normal(arg_keys[1], (D,), jnp.float32), 0.1, 1.9),
        "conv_first": noise(arg_keys[2], (27, D, D), (27 * D) ** -0.5, 0.0625, ((2, 16),)),
        "gain_second": jnp.clip(1.0 + 0.18 * jax.random.normal(arg_keys[3], (D,), jnp.float32), 0.1, 1.9),
        "conv_second": noise(arg_keys[4], (27, D, D), (27 * D) ** -0.5, 0.0625, ((2, 16),)),
        "gain_attn": jnp.clip(1.0 + 0.18 * jax.random.normal(arg_keys[5], (D,), jnp.float32), 0.1, 1.9),
        "w_qkv": draw_w_qkv(jax.random.fold_in(arg_keys[8], 71), 0),
        "w_proj": noise(arg_keys[7], (D, D), D ** -0.5, 0.3125),
    }


def rms_norm(values, gain):
    wide = values.astype(jnp.float32)
    return wide * lax.rsqrt(lax.optimization_barrier(jnp.mean(wide * wide, axis=-1, keepdims=True)) + 1e-06) * gain.astype(jnp.float32)

def causal_conv(active, weight):
    frames, rows, cols = (active.shape[0], active.shape[1], active.shape[2])
    padded = jnp.pad(active.astype(jnp.float32), ((2, 0), (1, 1), (1, 1), (0, 0)))
    filters = weight.astype(jnp.float32)
    total = jnp.zeros((frames, rows, cols, weight.shape[2]), jnp.float32)
    for tap in range(27):
        first, second, third = (tap // 9, tap // 3 % 3, tap % 3)
        window = padded[first:first + frames, second:second + rows, third:third + cols]
        total = total + jnp.einsum('fhwc,cd->fhwd', window, filters[tap])
    return total

def frame_attention(query, keys, values):
    scale = query.shape[-1] ** (-0.5)
    scores = jnp.dot(query, keys.T, preferred_element_type=jnp.float32) * scale
    top = lax.optimization_barrier(jnp.max(scores, axis=-1, keepdims=True))
    weights = jnp.exp(scores - top)
    total = lax.optimization_barrier(jnp.sum(weights, axis=-1, keepdims=True))
    summed = jnp.dot(weights.astype(jnp.bfloat16), values, preferred_element_type=jnp.float32)
    return (summed / total).astype(jnp.bfloat16)

def reference(video, gain_first, conv_first, gain_second, conv_second, gain_attn, w_qkv, w_proj):
    first = jax.nn.silu(rms_norm(video, gain_first)).astype(jnp.bfloat16)
    inner = causal_conv(first, conv_first)
    second = jax.nn.silu(rms_norm(inner, gain_second)).astype(jnp.bfloat16)
    block = (video.astype(jnp.float32) + causal_conv(second, conv_second)).astype(jnp.bfloat16)
    normed = rms_norm(block, gain_attn).astype(jnp.bfloat16)
    cells = HEIGHT * WIDTH
    qkv = jnp.dot(normed.reshape(FRAMES * cells, D), w_qkv, preferred_element_type=jnp.float32)
    qkv = qkv.astype(jnp.bfloat16).reshape(FRAMES, cells, 3 * D)
    attended = lax.map(lambda frame: frame_attention(frame[:, :D], frame[:, D:2 * D], frame[:, 2 * D:]), qkv)
    projected = jnp.dot(attended.reshape(FRAMES * cells, D), w_proj, preferred_element_type=jnp.float32)
    decoded = block.astype(jnp.float32) + projected.reshape(FRAMES, HEIGHT, WIDTH, D)
    return decoded.astype(jnp.bfloat16)
```

```python
import functools

import jax
import jax.numpy as jnp
from jax import lax
from jax.experimental import pallas as pl
from jax.experimental.pallas import tpu as pltpu
from jax.sharding import PartitionSpec as P

D = 384
BF = jnp.bfloat16
F32 = jnp.float32
NT = (((1,), (1,)), ((), ()))
NN = (((1,), (0,)), ((), ()))


def dot_nt(a, b):
    return lax.dot_general(a, b, NT, preferred_element_type=F32)


def dot_nn(a, b):
    return lax.dot_general(a, b, NN, preferred_element_type=F32)


def norm(wide, gain):
    return wide * lax.rsqrt(jnp.mean(wide * wide, axis=-1, keepdims=True) + 1e-06) * gain


def silu(v):
    return v / (1.0 + jnp.exp(-v))


def beside(x, axis, by):
    length = lax.axis_size(axis)
    pairs = [(i, i + by) for i in range(length) if 0 <= i + by < length]
    return lax.ppermute(x, axis, pairs)


def around(x, axis, by):
    length = lax.axis_size(axis)
    return lax.ppermute(x, axis, [(i, (i + by) % length) for i in range(length)])


def wide_halo(video):
    x = jnp.concatenate([beside(video[-4:], "ta", 1), video], axis=0)
    for axis, dim in (("ha", 1), ("wa", 2)):
        length = x.shape[dim]
        before = beside(lax.slice_in_dim(x, length - 2, length, axis=dim), axis, 1)
        after = beside(lax.slice_in_dim(x, 0, 2, axis=dim), axis, -1)
        x = jnp.concatenate([before, x, after], axis=dim)
    return x


def conv1_kernel(x_ref, e_ref, w_ref, gain_ref, mask_ref, emask_ref, out_ref, acc, eacc, joined):
    step = pl.program_id(0)
    j = step // 3
    k = step % 3
    total = None
    for i in range(3):
        part = dot_nt(x_ref[i, pl.ds(j, 10), pl.ds(k, 7)].reshape(1120, D), w_ref[i, 0])
        total = part if total is None else total + part
    etotal = None
    for i in range(3):
        part = dot_nt(e_ref[0, :, i * D:(i + 1) * D], w_ref[i, 0])
        etotal = part if etotal is None else etotal + part

    @pl.when(step == 0)
    def _():
        acc[...] = total
        eacc[...] = etotal

    @pl.when(step > 0)
    def _():
        acc[...] += total
        eacc[...] += etotal

    @pl.when(step == 8)
    def _():
        gain = gain_ref[...]
        second = silu(norm(acc[...], gain)) * mask_ref[...]
        joined[:, 2:18, :] = second.reshape(70, 16, D)
        extra = silu(norm(eacc[...], gain)) * emask_ref[...]
        joined[:, 0, :] = extra[0:70]
        joined[:, 1, :] = extra[72:142]
        for i in range(3):
            out_ref[i] = joined[:, i:i + 16, :].reshape(10, 7, 16, D).astype(BF)


def conv1(x, e, w, gain, mask, emask):
    return pl.pallas_call(
        conv1_kernel,
        grid=(9,),
        in_specs=[
            pl.BlockSpec((3, 12, 9, 16, D), lambda s: (0, 0, 0, 0, 0)),
            pl.BlockSpec((1, 144, 3 * D), lambda s: (s, 0, 0)),
            pl.BlockSpec((3, 1, D, D), lambda s: (0, s, 0, 0)),
            pl.BlockSpec((1, D), lambda s: (0, 0)),
            pl.BlockSpec((1120, 1), lambda s: (0, 0)),
            pl.BlockSpec((144, 1), lambda s: (0, 0)),
        ],
        out_specs=pl.BlockSpec((3, 10, 7, 16, D), lambda s: (0, 0, 0, 0, 0)),
        out_shape=jax.ShapeDtypeStruct((3, 10, 7, 16, D), BF),
        scratch_shapes=[
            pltpu.VMEM((1120, D), F32),
            pltpu.VMEM((144, D), F32),
            pltpu.VMEM((70, 24, D), F32),
        ],
        compiler_params=pltpu.CompilerParams(vmem_limit_bytes=48 * 2**20),
        name="conv1",
    )(x, e, w, gain, mask, emask)


def conv2_kernel(x_ref, w_ref, video_ref, out_ref, acc):
    step = pl.program_id(0)
    j = step // 3
    k = step % 3
    total = None
    for i in range(3):
        part = dot_nt(x_ref[i, pl.ds(j, 8), pl.ds(k, 5)].reshape(640, D), w_ref[i, 0])
        total = part if total is None else total + part

    @pl.when(step == 0)
    def _():
        acc[...] = total.reshape(40, 16, D)

    @pl.when(step > 0)
    def _():
        acc[...] += total.reshape(40, 16, D)

    @pl.when(step == 8)
    def _():
        for f in range(16):
            out_ref[f] = (video_ref[f].astype(F32) + acc[:, f, :]).astype(BF)


def conv2(x, w, video):
    return pl.pallas_call(
        conv2_kernel,
        grid=(9,),
        in_specs=[
            pl.BlockSpec((3, 10, 7, 16, D), lambda s: (0, 0, 0, 0, 0)),
            pl.BlockSpec((3, 1, D, D), lambda s: (0, s, 0, 0)),
            pl.BlockSpec((16, 40, D), lambda s: (0, 0, 0)),
        ],
        out_specs=pl.BlockSpec((16, 40, D), lambda s: (0, 0, 0)),
        out_shape=jax.ShapeDtypeStruct((16, 40, D), BF),
        scratch_shapes=[pltpu.VMEM((40, 16, D), F32)],
        compiler_params=pltpu.CompilerParams(vmem_limit_bytes=48 * 2**20),
        name="conv2",
    )(x, w, video)


def norm_kernel(block_ref, gain_ref, out_ref):
    out_ref[...] = norm(block_ref[...].astype(F32), gain_ref[...]).astype(BF)


def own_kernel(n_ref, w_ref, asked_ref, top_ref, total_ref, summed_ref):
    own = n_ref[...]
    query = dot_nn(own, w_ref[:, :D]).astype(BF)
    asked = (dot_nt(query, w_ref[:, D:2 * D]) * (D ** -0.5 * 1.4426950408889634)).astype(BF)
    asked_ref[...] = asked
    scores = dot_nt(asked, own)
    top = jnp.max(scores, axis=-1, keepdims=True)
    weights = jnp.exp2(scores - top)
    top_ref[...] = top
    total_ref[...] = jnp.sum(weights, axis=-1, keepdims=True)
    summed_ref[...] = dot_nn(weights.astype(BF), own)


def fold(asked, keys, top, total, summed):
    scores = [dot_nt(asked, k) for k in keys]
    new_top = top
    for s in scores:
        new_top = jnp.maximum(new_top, jnp.max(s, axis=-1, keepdims=True))
    rescale = jnp.exp2(top - new_top)
    total = total * rescale
    summed = summed * rescale
    for s, k in zip(scores, keys):
        weights = jnp.exp2(s - new_top)
        total = total + jnp.sum(weights, axis=-1, keepdims=True)
        summed = summed + dot_nn(weights.astype(BF), k)
    return new_top, total, summed


def mid_kernel(asked_ref, left_ref, right_ref, top_in, total_in, summed_in, top_ref, total_ref, summed_ref):
    top, total, summed = fold(
        asked_ref[...], [left_ref[...], right_ref[...]], top_in[...], total_in[...], summed_in[...]
    )
    top_ref[...] = top
    total_ref[...] = total
    summed_ref[...] = summed


def last_kernel(asked_ref, far_ref, top_in, total_in, summed_in, w_ref, proj_ref, block_ref, out_ref):
    _, total, summed = fold(asked_ref[...], [far_ref[...]], top_in[...], total_in[...], summed_in[...])
    mixed = (summed / total).astype(BF)
    attended = dot_nn(mixed, w_ref[:, 2 * D:]).astype(BF)
    out_ref[...] = (block_ref[...].astype(F32) + dot_nn(attended, proj_ref[...])).astype(BF)


def whole(kernel, outs, name):
    return pl.pallas_call(
        kernel,
        out_shape=outs,
        compiler_params=pltpu.CompilerParams(vmem_limit_bytes=48 * 2**20),
        name=name,
    )


def per_device(video, gain_first, conv_first, gain_second, conv_second, gain_attn, w_qkv, w_proj):
    w1 = lax.all_gather(jnp.swapaxes(conv_first, 1, 2), "wa", axis=1, tiled=True).reshape(3, 9, D, D)
    w2 = lax.all_gather(jnp.swapaxes(conv_second, 1, 2), "wa", axis=1, tiled=True).reshape(3, 9, D, D)

    first = silu(norm(wide_halo(video).astype(F32), gain_first)).astype(BF)
    turned = jnp.transpose(first, (1, 2, 0, 3))
    x = jnp.stack([turned[:, :, 2 + i:18 + i] for i in range(3)])
    e = jnp.stack([
        jnp.concatenate([first[i:i + 2, j:j + 10, k:k + 7].reshape(2, 70, D) for i in range(3)], axis=-1)
        for j in range(3) for k in range(3)
    ])
    e = jnp.pad(e, ((0, 0), (0, 0), (0, 2), (0, 0))).reshape(9, 144, 3 * D)

    ta, ha, wa = (lax.axis_index(n) for n in ("ta", "ha", "wa"))
    row = ha * 8 - 1 + jnp.arange(10)
    col = wa * 5 - 1 + jnp.arange(7)
    inside = ((row >= 0) & (row < 8 * lax.axis_size("ha")))[:, None] & ((col >= 0) & (col < 5 * lax.axis_size("wa")))
    inside = inside.astype(F32).reshape(70)
    mask = jnp.repeat(inside, 16).reshape(1120, 1)
    late = jnp.pad(inside, (0, 2)) * (ta > 0).astype(F32)
    emask = jnp.concatenate([late, late]).reshape(144, 1)

    second = conv1(x, e, w1, gain_second.reshape(1, D), mask, emask)
    block = conv2(second, w2, video.reshape(16, 40, D))
    strip = lax.all_to_all(block, "wa", split_axis=0, concat_axis=0, tiled=True).reshape(640, D)

    own = whole(norm_kernel, jax.ShapeDtypeStruct((640, D), BF), "norm")(strip, gain_attn.reshape(1, D))
    right = around(own, "ha", 1)
    left = around(own, "ha", -1)
    far = around(own, "ha", 2)
    stats = [jax.ShapeDtypeStruct((640, 1), F32), jax.ShapeDtypeStruct((640, 1), F32), jax.ShapeDtypeStruct((640, D), F32)]
    asked, *carry = whole(own_kernel, [jax.ShapeDtypeStruct((640, D), BF)] + stats, "own")(own, w_qkv)
    carry = whole(mid_kernel, stats, "mid")(asked, left, right, *carry)
    out = whole(last_kernel, jax.ShapeDtypeStruct((640, D), BF), "last")(asked, far, *carry, w_qkv, w_proj, strip)
    out = jnp.transpose(out.reshape(16, 8, 5, D), (1, 0, 2, 3))
    return out.reshape(1, 8, 80, D)


def solution(mesh):
    return jax.shard_map(
        per_device,
        mesh=mesh,
        in_specs=(
            P("ta", "ha", "wa", None),
            P(),
            P(None, None, "wa"),
            P(),
            P(None, None, "wa"),
            P(),
            P(),
            P(),
        ),
        out_specs=P(("ta", "wa"), "ha", None, None),
        check_vma=False,
    )
```

```python
import functools

import jax
import jax.numpy as jnp
from jax import lax
from jax.experimental import pallas as pl
from jax.experimental.pallas import tpu as pltpu
from jax.sharding import PartitionSpec as P

D = 384
BF = jnp.bfloat16
F32 = jnp.float32
NT = (((1,), (1,)), ((), ()))
NN = (((1,), (0,)), ((), ()))


def dot_nt(a, b):
    return lax.dot_general(a, b, NT, preferred_element_type=F32)


def dot_nn(a, b):
    return lax.dot_general(a, b, NN, preferred_element_type=F32)


def norm(wide, gain):
    return wide * lax.rsqrt(jnp.mean(wide * wide, axis=-1, keepdims=True) + 1e-06) * gain


def silu(v):
    return v / (1.0 + jnp.exp(-v))


def beside(x, axis, by):
    length = lax.axis_size(axis)
    pairs = [(i, i + by) for i in range(length) if 0 <= i + by < length]
    return lax.ppermute(x, axis, pairs)


def around(x, axis, by):
    length = lax.axis_size(axis)
    return lax.ppermute(x, axis, [(i, (i + by) % length) for i in range(length)])


def wide_halo(video):
    x = jnp.concatenate([beside(video[-4:], "ta", 1), video], axis=0)
    for axis, dim in (("ha", 1), ("wa", 2)):
        length = x.shape[dim]
        before = beside(lax.slice_in_dim(x, length - 2, length, axis=dim), axis, 1)
        after = beside(lax.slice_in_dim(x, 0, 2, axis=dim), axis, -1)
        x = jnp.concatenate([before, x, after], axis=dim)
    return x


def fixed(*shape):
    return pl.BlockSpec(shape, lambda s: (0,) * len(shape))


def conv1_kernel(x_ref, e_ref, w_ref, gain_ref, mask_ref, emask_ref, out_ref, acc, eacc, joined):
    step = pl.program_id(0)
    windows, taps = [], []
    for k in range(3):
        for i in range(3):
            windows.append(x_ref[i, pl.ds(step, 10), k:k + 7].reshape(1120, D))
            taps.append(w_ref[3 * k + i])
    taps = jnp.concatenate(taps, axis=1)
    total = dot_nt(jnp.concatenate(windows, axis=1), taps)
    etotal = dot_nt(e_ref[0], taps)

    @pl.when(step == 0)
    def _():
        acc[...] = total
        eacc[...] = etotal

    @pl.when(step == 1)
    def _():
        acc[...] += total
        eacc[...] += etotal

    @pl.when(step == 2)
    def _():
        gain = gain_ref[...]
        second = (silu(norm(acc[...] + total, gain)) * mask_ref[...]).reshape(70, 16, D)
        for row in range(10):
            joined[row * 9:row * 9 + 7, 2:18, :] = second[row * 7:row * 7 + 7]
        extra = silu(norm(eacc[...] + etotal, gain)) * emask_ref[...]
        joined[:, 0, :] = extra[0:90]
        joined[:, 1, :] = extra[96:186]
        for i in range(3):
            for row in range(10):
                out_ref[i, row] = joined[row * 9:row * 9 + 7, i:i + 16, :].astype(BF)


def conv1(x, e, w, gain, mask, emask):
    return pl.pallas_call(
        conv1_kernel,
        grid=(3,),
        in_specs=[
            fixed(3, 12, 9, 16, D),
            pl.BlockSpec((1, 192, 9 * D), lambda s: (s, 0, 0)),
            pl.BlockSpec((9, D, D), lambda s: (s, 0, 0)),
            fixed(1, D), fixed(1120, 1), fixed(192, 1),
        ],
        out_specs=fixed(3, 10, 7, 16, D),
        out_shape=jax.ShapeDtypeStruct((3, 10, 7, 16, D), BF),
        scratch_shapes=[
            pltpu.VMEM((1120, D), F32),
            pltpu.VMEM((192, D), F32),
            pltpu.VMEM((90, 24, D), F32),
        ],
        compiler_params=pltpu.CompilerParams(vmem_limit_bytes=56 * 2**20),
        name="conv1",
    )(x, e, w, gain, mask, emask)


def window2(x_ref, tap):
    i, j, k = tap // 9, tap // 3 % 3, tap % 3
    return x_ref[i, pl.ds(j, 8), pl.ds(k, 5)].reshape(640, D)


def conv2_begin_kernel(core_ref, x_ref, mine_ref, other_ref, acc_ref):
    step = pl.program_id(0)
    core = core_ref[0]
    windows, taps = [], []
    for at in range(4):
        windows.append(window2(x_ref, 4 * step + at))
        mine, other = mine_ref[at], other_ref[at]
        taps.append(jnp.concatenate([jnp.where(core == 0, mine, other), jnp.where(core == 0, other, mine)], axis=0))
    total = dot_nt(jnp.concatenate(windows, axis=1), jnp.concatenate(taps, axis=1)).reshape(40, 16, D)

    @pl.when(step == 0)
    def _():
        acc_ref[...] = total

    @pl.when(step > 0)
    def _():
        acc_ref[...] += total


def conv2_begin(core, x, mine, other):
    half = pl.BlockSpec((4, D // 2, D), lambda s, core: (s, 0, 0))
    return pl.pallas_call(
        conv2_begin_kernel,
        grid_spec=pltpu.PrefetchScalarGridSpec(
            num_scalar_prefetch=1,
            grid=(4,),
            in_specs=[pl.BlockSpec((3, 10, 7, 16, D), lambda s, core: (0, 0, 0, 0, 0)), half, half],
            out_specs=pl.BlockSpec((40, 16, D), lambda s, core: (0, 0, 0)),
        ),
        out_shape=jax.ShapeDtypeStruct((40, 16, D), F32),
        compiler_params=pltpu.CompilerParams(vmem_limit_bytes=56 * 2**20),
        name="conv2_begin",
    )(core, x, mine, other)


def conv2_end_kernel(x_ref, w_ref, acc_in, video_ref, out_ref, acc):
    windows = [window2(x_ref, tap) for tap in range(ROUND, 27)]
    taps = [w_ref[n] for n in range(27 - ROUND)]
    total = dot_nt(jnp.concatenate(windows, axis=1), jnp.concatenate(taps, axis=1))
    acc[...] = acc_in[...] + total.reshape(40, 16, D)
    for f in range(16):
        out_ref[f] = (video_ref[f].astype(F32) + acc[:, f, :]).astype(BF)


def conv2_end(x, w, acc, video):
    return pl.pallas_call(
        conv2_end_kernel,
        out_shape=jax.ShapeDtypeStruct((16, 40, D), BF),
        scratch_shapes=[pltpu.VMEM((40, 16, D), F32)],
        compiler_params=pltpu.CompilerParams(vmem_limit_bytes=56 * 2**20),
        name="conv2_end",
    )(x, w, acc, video)


ROUND = 16


def own_half(shard, ta, ha, core):
    taken = lax.dynamic_index_in_dim(shard, ta * 4 + ha, 0, keepdims=False)
    sent = jnp.broadcast_to(taken[None], (16, 24, D))
    tap = lax.all_to_all(sent, "wa", split_axis=0, concat_axis=0, tiled=True).reshape(2, D // 2, D)
    return lax.dynamic_index_in_dim(tap, core, 0, keepdims=False)


def over_torus(half):
    sent = jnp.broadcast_to(half[None], (16, D // 2, D))
    return lax.all_to_all(sent, ("ta", "ha"), split_axis=0, concat_axis=0, tiled=True)


def swapped(x):
    length = lax.axis_size("wa")
    return lax.ppermute(x, "wa", [(i, i ^ 1) for i in range(length)])


def norm_kernel(block_ref, gain_ref, out_ref):
    out_ref[...] = norm(block_ref[...].astype(F32), gain_ref[...]).astype(BF)


def own_kernel(n_ref, w_ref, asked_ref, top_ref, total_ref, summed_ref):
    own = n_ref[...]
    query = dot_nn(own, w_ref[:, :D]).astype(BF)
    asked = (dot_nt(query, w_ref[:, D:2 * D]) * (D ** -0.5 * 1.4426950408889634)).astype(BF)
    asked_ref[...] = asked
    scores = dot_nt(asked, own)
    top = jnp.max(scores, axis=-1, keepdims=True)
    weights = jnp.exp2(scores - top)
    top_ref[...] = top
    total_ref[...] = jnp.sum(weights, axis=-1, keepdims=True)
    summed_ref[...] = dot_nn(weights.astype(BF), own)


def fold(asked, keys, top, total, summed):
    scores = [dot_nt(asked, k) for k in keys]
    new_top = top
    for s in scores:
        new_top = jnp.maximum(new_top, jnp.max(s, axis=-1, keepdims=True))
    rescale = jnp.exp2(top - new_top)
    total = total * rescale
    summed = summed * rescale
    for s, k in zip(scores, keys):
        weights = jnp.exp2(s - new_top)
        total = total + jnp.sum(weights, axis=-1, keepdims=True)
        summed = summed + dot_nn(weights.astype(BF), k)
    return new_top, total, summed


def mid_kernel(asked_ref, left_ref, right_ref, top_in, total_in, summed_in, top_ref, total_ref, summed_ref):
    top, total, summed = fold(
        asked_ref[...], [left_ref[...], right_ref[...]], top_in[...], total_in[...], summed_in[...]
    )
    top_ref[...] = top
    total_ref[...] = total
    summed_ref[...] = summed


def last_kernel(asked_ref, far_ref, top_in, total_in, summed_in, w_ref, proj_ref, block_ref, out_ref):
    _, total, summed = fold(asked_ref[...], [far_ref[...]], top_in[...], total_in[...], summed_in[...])
    mixed = (summed / total).astype(BF)
    attended = dot_nn(mixed, w_ref[:, 2 * D:]).astype(BF)
    out_ref[...] = (block_ref[...].astype(F32) + dot_nn(attended, proj_ref[...])).astype(BF)


def whole(kernel, outs, name):
    return pl.pallas_call(
        kernel,
        out_shape=outs,
        compiler_params=pltpu.CompilerParams(vmem_limit_bytes=48 * 2**20),
        name=name,
    )


def per_device(video, gain_first, conv_first, gain_second, conv_second, gain_attn, w_qkv, w_proj):
    ta, ha, wa = (lax.axis_index(n) for n in ("ta", "ha", "wa"))
    core = wa % 2
    shard1 = jnp.swapaxes(conv_first, 1, 2).reshape(3, 9, 24, D)
    shard1 = jnp.swapaxes(shard1, 0, 1).reshape(27, 24, D)
    filter1 = lax.all_gather(shard1, "wa", axis=1, tiled=True)
    shard2 = jnp.swapaxes(conv_second, 1, 2)
    kept = lax.all_gather(shard2[ROUND:], "wa", axis=1, tiled=True)
    mine = over_torus(own_half(shard2, ta, ha, core))

    first = silu(norm(wide_halo(video).astype(F32), gain_first)).astype(BF)
    turned = jnp.transpose(first, (1, 2, 0, 3))
    x = jnp.stack([turned[:, :, 2 + i:18 + i] for i in range(3)])
    flat = jnp.pad(first[:4].reshape(4, 108, D), ((0, 0), (0, 8), (0, 0)))
    e = jnp.stack([
        jnp.concatenate([flat[i:i + 2, 9 * j + k:9 * j + k + 96] for k in range(3) for i in range(3)], axis=-1)
        for j in range(3)
    ]).reshape(3, 192, 9 * D)

    row = ha * 8 - 1 + jnp.arange(10)
    col = wa * 5 - 1 + jnp.arange(7)
    inside = ((row >= 0) & (row < 8 * lax.axis_size("ha")))[:, None] & ((col >= 0) & (col < 5 * lax.axis_size("wa")))
    inside = inside.astype(F32).reshape(70)
    mask = jnp.repeat(inside, 16).reshape(1120, 1)
    late = jnp.pad(inside.reshape(10, 7), ((0, 0), (0, 2))).reshape(90) * (ta > 0).astype(F32)
    emask = jnp.concatenate([jnp.pad(late, (0, 6))] * 2).reshape(192, 1)

    second = conv1(x, e, filter1, gain_second.reshape(1, D), mask, emask)
    second, mine = lax.optimization_barrier((second, mine))
    acc = conv2_begin(core.reshape(1).astype(jnp.int32), second, mine, swapped(mine))
    block = conv2_end(second, kept, acc, video.reshape(16, 40, D))
    strip = lax.all_to_all(block, "wa", split_axis=0, concat_axis=0, tiled=True).reshape(640, D)

    own = whole(norm_kernel, jax.ShapeDtypeStruct((640, D), BF), "norm")(strip, gain_attn.reshape(1, D))
    right = around(own, "ha", 1)
    left = around(own, "ha", -1)
    stats = [jax.ShapeDtypeStruct((640, 1), F32), jax.ShapeDtypeStruct((640, 1), F32), jax.ShapeDtypeStruct((640, D), F32)]
    asked, *carry = whole(own_kernel, [jax.ShapeDtypeStruct((640, D), BF)] + stats, "own")(own, w_qkv)
    asked, own = lax.optimization_barrier((asked, own))
    far = around(own, "ha", 2)
    carry = whole(mid_kernel, stats, "mid")(asked, left, right, *carry)
    out = whole(last_kernel, jax.ShapeDtypeStruct((640, D), BF), "last")(asked, far, *carry, w_qkv, w_proj, strip)
    out = jnp.transpose(out.reshape(16, 8, 5, D), (1, 0, 2, 3))
    return out.reshape(1, 8, 80, D)


def solution(mesh):
    return jax.shard_map(
        per_device,
        mesh=mesh,
        in_specs=(
            P("ta", "ha", "wa", None),
            P(),
            P(None, None, "wa"),
            P(),
            P(None, None, "wa"),
            P(),
            P(),
            P(),
        ),
        out_specs=P(("ta", "wa"), "ha", None, None),
        check_vma=False,
    )
```

```python
import functools

import jax
import jax.numpy as jnp
from jax import lax
from jax.experimental import pallas as pl
from jax.experimental.pallas import tpu as pltpu
from jax.sharding import PartitionSpec as P

D = 384
BF = jnp.bfloat16
F32 = jnp.float32
NT = (((1,), (1,)), ((), ()))
NN = (((1,), (0,)), ((), ()))


def dot_nt(a, b):
    return lax.dot_general(a, b, NT, preferred_element_type=F32)


def dot_nn(a, b):
    return lax.dot_general(a, b, NN, preferred_element_type=F32)


def norm(wide, gain):
    return wide * lax.rsqrt(jnp.mean(wide * wide, axis=-1, keepdims=True) + 1e-06) * gain


def silu(v):
    return v / (1.0 + jnp.exp(-v))


def beside(x, axis, by):
    length = lax.axis_size(axis)
    pairs = [(i, i + by) for i in range(length) if 0 <= i + by < length]
    return lax.ppermute(x, axis, pairs)


def around(x, axis, by):
    length = lax.axis_size(axis)
    return lax.ppermute(x, axis, [(i, (i + by) % length) for i in range(length)])


def rims(x, dim):
    length = x.shape[dim]
    return lax.slice_in_dim(x, length - 2, length, axis=dim), lax.slice_in_dim(x, 0, 2, axis=dim)


def halo(x, axis, dim):
    late, early = rims(x, dim)
    return jnp.concatenate([beside(late, axis, 1), x, beside(early, axis, -1)], axis=dim)


def fixed(*shape):
    return pl.BlockSpec(shape, lambda s: (0,) * len(shape))


def prepare_kernel(wide_ref, gain_ref, x_ref, e_ref, turned, flat):
    gain = gain_ref[...]
    for row in range(12):
        cells = slice(row * 9, row * 9 + 9)
        turned[cells, 0:20, :] = silu(norm(wide_ref[cells].astype(F32), gain))
        for i in range(3):
            x_ref[i, row] = turned[cells, 2 + i:18 + i, :].astype(BF)
    for f in range(4):
        flat[f, 0:108, :] = turned[:, f, :]
        flat[f, 108:128, :] = jnp.zeros((20, D), F32)
    for j in range(3):
        for k in range(3):
            for i in range(3):
                for f in range(2):
                    e_ref[9 * i + 3 * j + k, f * 96:f * 96 + 96, :] = (
                        flat[f + i, 9 * j + k:9 * j + k + 96, :].astype(BF)
                    )


def prepare(wide, gain):
    return pl.pallas_call(
        prepare_kernel,
        out_shape=[
            jax.ShapeDtypeStruct((3, 12, 9, 16, D), BF),
            jax.ShapeDtypeStruct((27, 192, D), BF),
        ],
        scratch_shapes=[pltpu.VMEM((108, 24, D), F32), pltpu.VMEM((4, 128, D), F32)],
        compiler_params=pltpu.CompilerParams(vmem_limit_bytes=56 * 2**20),
        name="prepare",
    )(wide, gain)


ROUND = 15


def window(x_ref, tap, rows, cols):
    i, j, k = tap // 9, tap // 3 % 3, tap % 3
    return x_ref[i, pl.ds(j, rows), pl.ds(k, cols)].reshape(rows * cols * 16, D)


def conv1_taps(x_ref, e_ref, start, taps):
    windows = [window(x_ref, start + n, 10, 7) for n in range(len(taps))]
    extras = [e_ref[n] for n in range(len(taps))]
    taps = jnp.concatenate(taps, axis=1)
    return dot_nt(jnp.concatenate(windows, axis=1), taps), dot_nt(jnp.concatenate(extras, axis=1), taps)


def conv1_begin_kernel(x_ref, e_ref, w_ref, acc_ref, eacc_ref):
    step = pl.program_id(0)
    total, etotal = conv1_taps(x_ref, e_ref, ROUND + 3 * step, [w_ref[n] for n in range(3)])

    @pl.when(step == 0)
    def _():
        acc_ref[...] = total
        eacc_ref[...] = etotal

    @pl.when(step > 0)
    def _():
        acc_ref[...] += total
        eacc_ref[...] += etotal


def conv1_begin(x, e, w):
    return pl.pallas_call(
        conv1_begin_kernel,
        grid=(4,),
        in_specs=[
            fixed(3, 12, 9, 16, D),
            pl.BlockSpec((3, 192, D), lambda s: (s + ROUND // 3, 0, 0)),
            pl.BlockSpec((3, D, D), lambda s: (s, 0, 0)),
        ],
        out_specs=[fixed(1120, D), fixed(192, D)],
        out_shape=[jax.ShapeDtypeStruct((1120, D), F32), jax.ShapeDtypeStruct((192, D), F32)],
        compiler_params=pltpu.CompilerParams(vmem_limit_bytes=56 * 2**20),
        name="conv1_begin",
    )(x, e, w)


def conv1_end_kernel(
    core_ref, x_ref, e_ref, mine_ref, other_ref, acc_in, eacc_in, gain_ref, mask_ref, emask_ref, out_ref, acc, eacc, joined
):
    step = pl.program_id(0)
    first = core_ref[0] == 0
    taps = []
    for n in range(5):
        mine, other = mine_ref[n], other_ref[n]
        taps.append(jnp.concatenate([jnp.where(first, mine, other), jnp.where(first, other, mine)], axis=0))
    total, etotal = conv1_taps(x_ref, e_ref, 5 * step, taps)

    @pl.when(step == 0)
    def _():
        acc[...] = acc_in[...] + total
        eacc[...] = eacc_in[...] + etotal

    @pl.when(step == 1)
    def _():
        acc[...] += total
        eacc[...] += etotal

    @pl.when(step == 2)
    def _():
        gain = gain_ref[...]
        second = (silu(norm(acc[...] + total, gain)) * mask_ref[...]).reshape(70, 16, D)
        for row in range(10):
            joined[row * 9:row * 9 + 7, 2:18, :] = second[row * 7:row * 7 + 7]
        extra = silu(norm(eacc[...] + etotal, gain)) * emask_ref[...]
        joined[:, 0, :] = extra[0:90]
        joined[:, 1, :] = extra[96:186]
        for i in range(3):
            for row in range(10):
                out_ref[i, row] = joined[row * 9:row * 9 + 7, i:i + 16, :].astype(BF)


def conv1_end(core, x, e, mine, other, acc, eacc, gain, mask, emask):
    half = pl.BlockSpec((5, D // 2, D), lambda s: (s, 0, 0))
    return pl.pallas_call(
        conv1_end_kernel,
        grid=(3,),
        in_specs=[
            pl.BlockSpec(memory_space=pltpu.SMEM),
            fixed(3, 12, 9, 16, D),
            pl.BlockSpec((5, 192, D), lambda s: (s, 0, 0)),
            half, half, fixed(1120, D), fixed(192, D), fixed(1, D), fixed(1120, 1), fixed(192, 1),
        ],
        out_specs=fixed(3, 10, 7, 16, D),
        out_shape=jax.ShapeDtypeStruct((3, 10, 7, 16, D), BF),
        scratch_shapes=[
            pltpu.VMEM((1120, D), F32),
            pltpu.VMEM((192, D), F32),
            pltpu.VMEM((90, 24, D), F32),
        ],
        compiler_params=pltpu.CompilerParams(vmem_limit_bytes=56 * 2**20),
        name="conv1_end",
    )(core, x, e, mine, other, acc, eacc, gain, mask, emask)


def conv2_kernel(x_ref, w_ref, video_ref, out_ref, acc):
    step = pl.program_id(0)
    windows, taps = [], []
    for k in range(3):
        for i in range(3):
            windows.append(x_ref[i, pl.ds(step, 8), k:k + 5].reshape(640, D))
            taps.append(w_ref[i, 0, k])
    total = dot_nt(jnp.concatenate(windows, axis=1), jnp.concatenate(taps, axis=1)).reshape(40, 16, D)

    @pl.when(step == 0)
    def _():
        acc[...] = total

    @pl.when(step > 0)
    def _():
        acc[...] += total

    @pl.when(step == 2)
    def _():
        for f in range(16):
            out_ref[f] = (video_ref[f].astype(F32) + acc[:, f, :]).astype(BF)


def conv2(x, w, video):
    return pl.pallas_call(
        conv2_kernel,
        grid=(3,),
        in_specs=[
            fixed(3, 10, 7, 16, D),
            pl.BlockSpec((3, 1, 3, D, D), lambda s: (0, s, 0, 0, 0)),
            fixed(16, 40, D),
        ],
        out_specs=fixed(16, 40, D),
        out_shape=jax.ShapeDtypeStruct((16, 40, D), BF),
        scratch_shapes=[pltpu.VMEM((40, 16, D), F32)],
        compiler_params=pltpu.CompilerParams(vmem_limit_bytes=56 * 2**20),
        name="conv2",
    )(x, w, video)


def own_tap(shard, ta, ha):
    taken = lax.dynamic_index_in_dim(shard, ta * 4 + ha, 0, keepdims=False)
    sent = jnp.broadcast_to(taken[None], (16, 24, D))
    return lax.all_to_all(sent, "wa", split_axis=0, concat_axis=0, tiled=True).reshape(2, D // 2, D)


def over_torus(half):
    sent = jnp.broadcast_to(half[None], (16, D // 2, D))
    return lax.all_to_all(sent, ("ta", "ha"), split_axis=0, concat_axis=0, tiled=True)


def swapped(x):
    length = lax.axis_size("wa")
    return lax.ppermute(x, "wa", [(i, i ^ 1) for i in range(length)])


def norm_kernel(block_ref, gain_ref, out_ref):
    out_ref[...] = norm(block_ref[...].astype(F32), gain_ref[...]).astype(BF)


def own_kernel(n_ref, w_ref, asked_ref, top_ref, total_ref, summed_ref):
    own = n_ref[...]
    query = dot_nn(own, w_ref[:, :D]).astype(BF)
    asked = (dot_nt(query, w_ref[:, D:2 * D]) * (D ** -0.5 * 1.4426950408889634)).astype(BF)
    asked_ref[...] = asked
    scores = dot_nt(asked, own)
    top = jnp.max(scores, axis=-1, keepdims=True)
    weights = jnp.exp2(scores - top)
    top_ref[...] = top
    total_ref[...] = jnp.sum(weights, axis=-1, keepdims=True)
    summed_ref[...] = dot_nn(weights.astype(BF), own)


def fold(asked, keys, top, total, summed):
    scores = [dot_nt(asked, k) for k in keys]
    new_top = top
    for s in scores:
        new_top = jnp.maximum(new_top, jnp.max(s, axis=-1, keepdims=True))
    rescale = jnp.exp2(top - new_top)
    total = total * rescale
    summed = summed * rescale
    for s, k in zip(scores, keys):
        weights = jnp.exp2(s - new_top)
        total = total + jnp.sum(weights, axis=-1, keepdims=True)
        summed = summed + dot_nn(weights.astype(BF), k)
    return new_top, total, summed


def mid_kernel(asked_ref, left_ref, right_ref, top_in, total_in, summed_in, top_ref, total_ref, summed_ref):
    top, total, summed = fold(
        asked_ref[...], [left_ref[...], right_ref[...]], top_in[...], total_in[...], summed_in[...]
    )
    top_ref[...] = top
    total_ref[...] = total
    summed_ref[...] = summed


def last_kernel(asked_ref, far0_ref, far1_ref, top_in, total_in, summed_in, w_ref, proj_ref, block_ref, out_ref):
    far = jnp.concatenate([far0_ref[...], far1_ref[...]], axis=0)
    _, total, summed = fold(asked_ref[...], [far], top_in[...], total_in[...], summed_in[...])
    mixed = (summed / total).astype(BF)
    attended = dot_nn(mixed, w_ref[:, 2 * D:]).astype(BF)
    out_ref[...] = (block_ref[...].astype(F32) + dot_nn(attended, proj_ref[...])).astype(BF)


def whole(kernel, outs, name):
    return pl.pallas_call(
        kernel,
        out_shape=outs,
        compiler_params=pltpu.CompilerParams(vmem_limit_bytes=48 * 2**20),
        name=name,
    )


def per_device(video, gain_first, conv_first, gain_second, conv_second, gain_attn, w_qkv, w_proj):
    ta, ha, wa = (lax.axis_index(n) for n in ("ta", "ha", "wa"))
    core = wa % 2
    shard1 = jnp.swapaxes(conv_first, 1, 2)
    kept = lax.all_gather(shard1[ROUND:], "wa", axis=1, tiled=True)
    filter2 = lax.all_gather(jnp.swapaxes(conv_second, 1, 2), "wa", axis=1, tiled=True).reshape(3, 3, 3, D, D)
    halves = own_tap(shard1, ta, ha)
    tall = halo(jnp.concatenate([beside(video[-4:], "ta", 1), video], axis=0), "ha", 1)
    sides = rims(tall, 2)
    halves, *_ = lax.optimization_barrier((halves, *sides))
    mine = over_torus(lax.dynamic_index_in_dim(halves, core, 0, keepdims=False))
    wide = jnp.concatenate([beside(sides[0], "wa", 1), tall, beside(sides[1], "wa", -1)], axis=2)
    x, e = prepare(jnp.transpose(wide, (1, 2, 0, 3)).reshape(108, 20, D), gain_first.reshape(1, D))

    row = ha * 8 - 1 + jnp.arange(10)
    col = wa * 5 - 1 + jnp.arange(7)
    inside = ((row >= 0) & (row < 8 * lax.axis_size("ha")))[:, None] & ((col >= 0) & (col < 5 * lax.axis_size("wa")))
    inside = inside.astype(F32).reshape(70)
    mask = jnp.repeat(inside, 16).reshape(1120, 1)
    late = jnp.pad(inside.reshape(10, 7), ((0, 0), (0, 2))).reshape(90) * (ta > 0).astype(F32)
    emask = jnp.concatenate([jnp.pad(late, (0, 6))] * 2).reshape(192, 1)

    acc, eacc = conv1_begin(x, e, kept)
    acc, mine = lax.optimization_barrier((acc, mine))
    second = conv1_end(
        core.reshape(1).astype(jnp.int32), x, e, mine, swapped(mine), acc, eacc, gain_second.reshape(1, D), mask, emask
    )
    block = conv2(second, filter2, video.reshape(16, 40, D))
    strip = lax.all_to_all(block, "wa", split_axis=0, concat_axis=0, tiled=True).reshape(640, D)

    own = whole(norm_kernel, jax.ShapeDtypeStruct((640, D), BF), "norm")(strip, gain_attn.reshape(1, D))
    right = around(own, "ha", 1)
    left = around(own, "ha", -1)
    stats = [jax.ShapeDtypeStruct((640, 1), F32), jax.ShapeDtypeStruct((640, 1), F32), jax.ShapeDtypeStruct((640, D), F32)]
    asked, *carry = whole(own_kernel, [jax.ShapeDtypeStruct((640, D), BF)] + stats, "own")(own, w_qkv)
    far0 = around(right[:320], "ha", 1)
    far1 = around(left[320:], "ha", -1)
    carry = whole(mid_kernel, stats, "mid")(asked, left, right, *carry)
    out = whole(last_kernel, jax.ShapeDtypeStruct((640, D), BF), "last")(asked, far0, far1, *carry, w_qkv, w_proj, strip)
    out = jnp.transpose(out.reshape(16, 8, 5, D), (1, 0, 2, 3))
    return out.reshape(1, 8, 80, D)


def solution(mesh):
    return jax.shard_map(
        per_device,
        mesh=mesh,
        in_specs=(
            P("ta", "ha", "wa", None),
            P(),
            P(None, None, "wa"),
            P(),
            P(None, None, "wa"),
            P(),
            P(),
            P(),
        ),
        out_specs=P(("ta", "wa"), "ha", None, None),
        check_vma=False,
    )
```

```python
import functools

import jax
import jax.numpy as jnp
from jax import lax
from jax.experimental import pallas as pl
from jax.experimental.pallas import tpu as pltpu
from jax.sharding import PartitionSpec as P

D = 384
ROUND = 11
ROUND2 = 16 - ROUND
BF = jnp.bfloat16
F32 = jnp.float32
NT = (((1,), (1,)), ((), ()))
NN = (((1,), (0,)), ((), ()))


def dot_nt(a, b):
    return lax.dot_general(a, b, NT, preferred_element_type=F32)


def dot_nn(a, b):
    return lax.dot_general(a, b, NN, preferred_element_type=F32)


def norm(wide, gain):
    return wide * lax.rsqrt(jnp.mean(wide * wide, axis=-1, keepdims=True) + 1e-06) * gain


def silu(v):
    return v / (1.0 + jnp.exp(-v))


def beside(x, axis, by):
    length = lax.axis_size(axis)
    pairs = [(i, i + by) for i in range(length) if 0 <= i + by < length]
    return lax.ppermute(x, axis, pairs)


def around(x, axis, by):
    length = lax.axis_size(axis)
    return lax.ppermute(x, axis, [(i, (i + by) % length) for i in range(length)])


def rims(x, dim):
    length = x.shape[dim]
    return lax.slice_in_dim(x, length - 2, length, axis=dim), lax.slice_in_dim(x, 0, 2, axis=dim)


def halo(x, axis, dim):
    late, early = rims(x, dim)
    return jnp.concatenate([beside(late, axis, 1), x, beside(early, axis, -1)], axis=dim)


def fixed(*shape):
    return pl.BlockSpec(shape, lambda s: (0,) * len(shape))


def prepare_kernel(before_ref, tall_ref, after_ref, gain_ref, x_ref, round_ref, kept_ref, turned, flat):
    gain = gain_ref[...]
    for row in range(12):
        cells = slice(row * 9, row * 9 + 9)
        for part, at, count in ((before_ref, 0, 2), (tall_ref, 2, 5), (after_ref, 7, 2)):
            turned[row * 9 + at:row * 9 + at + count, 0:20, :] = silu(
                norm(part[row * count:row * count + count].astype(F32), gain)
            )
        for i in range(3):
            x_ref[i, row] = turned[cells, 2 + i:18 + i, :].astype(BF)
    for f in range(4):
        flat[f, 0:108, :] = turned[:, f, :]
        flat[f, 108:128, :] = jnp.zeros((20, D), F32)
    for tap in range(27):
        i, j, k = tap // 9, tap // 3 % 3, tap % 3
        target, at = (round_ref, tap) if tap < ROUND else (kept_ref, tap - ROUND)
        for f in range(2):
            target[at, f * 96:f * 96 + 96, :] = flat[f + i, 9 * j + k:9 * j + k + 96, :].astype(BF)
    round_ref[ROUND] = jnp.zeros((192, D), BF)


def turn(x):
    return jnp.transpose(x, (1, 2, 0, 3)).reshape(-1, x.shape[0], D)


def prepare(before, tall, after, gain):
    return pl.pallas_call(
        prepare_kernel,
        out_shape=[
            jax.ShapeDtypeStruct((3, 12, 9, 16, D), BF),
            jax.ShapeDtypeStruct((ROUND + 1, 192, D), BF),
            jax.ShapeDtypeStruct((27 - ROUND, 192, D), BF),
        ],
        scratch_shapes=[pltpu.VMEM((108, 24, D), F32), pltpu.VMEM((4, 128, D), F32)],
        compiler_params=pltpu.CompilerParams(vmem_limit_bytes=56 * 2**20),
        name="prepare",
    )(before, tall, after, gain)


def window(x_ref, tap, rows, cols):
    i, j, k = tap // 9, tap // 3 % 3, tap % 3
    return x_ref[i, pl.ds(j, rows), pl.ds(k, cols)].reshape(rows * cols * 16, D)


def conv1_taps(x_ref, e_ref, start, taps):
    windows = [window(x_ref, start + n, 10, 7) for n in range(len(taps))]
    extras = [e_ref[n] for n in range(len(taps))]
    taps = jnp.concatenate(taps, axis=1)
    return dot_nt(jnp.concatenate(windows, axis=1), taps), dot_nt(jnp.concatenate(extras, axis=1), taps)


def conv1_begin_kernel(x_ref, e_ref, w_ref, acc_ref, eacc_ref):
    step = pl.program_id(0)
    total, etotal = conv1_taps(x_ref, e_ref, ROUND + 4 * step, [w_ref[n] for n in range(4)])

    @pl.when(step == 0)
    def _():
        acc_ref[...] = total
        eacc_ref[...] = etotal

    @pl.when(step > 0)
    def _():
        acc_ref[...] += total
        eacc_ref[...] += etotal


def conv1_begin(x, e, w):
    return pl.pallas_call(
        conv1_begin_kernel,
        grid=(4,),
        in_specs=[
            fixed(3, 12, 9, 16, D),
            pl.BlockSpec((4, 192, D), lambda s: (s, 0, 0)),
            pl.BlockSpec((4, D, D), lambda s: (s, 0, 0)),
        ],
        out_specs=[fixed(1120, D), fixed(192, D)],
        out_shape=[jax.ShapeDtypeStruct((1120, D), F32), jax.ShapeDtypeStruct((192, D), F32)],
        compiler_params=pltpu.CompilerParams(vmem_limit_bytes=56 * 2**20),
        name="conv1_begin",
    )(x, e, w)


def joint(core_ref, mine, other):
    first = core_ref[0] == 0
    return jnp.concatenate([jnp.where(first, mine, other), jnp.where(first, other, mine)], axis=0)


def conv1_end_kernel(
    core_ref, x_ref, e_ref, mine_ref, other_ref, acc_in, eacc_in, gain_ref, mask_ref, emask_ref, out_ref, acc, eacc, joined
):
    step = pl.program_id(0)
    taps = [joint(core_ref, mine_ref[n], other_ref[n]) for n in range(4)]
    taps[3] = jnp.where(step == 2, jnp.zeros_like(taps[3]), taps[3])
    total, etotal = conv1_taps(x_ref, e_ref, 4 * step, taps)

    @pl.when(step == 0)
    def _():
        acc[...] = acc_in[...] + total
        eacc[...] = eacc_in[...] + etotal

    @pl.when(step == 1)
    def _():
        acc[...] += total
        eacc[...] += etotal

    @pl.when(step == 2)
    def _():
        gain = gain_ref[...]
        second = (silu(norm(acc[...] + total, gain)) * mask_ref[...]).reshape(70, 16, D)
        for row in range(10):
            joined[row * 9:row * 9 + 7, 2:18, :] = second[row * 7:row * 7 + 7]
        extra = silu(norm(eacc[...] + etotal, gain)) * emask_ref[...]
        joined[:, 0, :] = extra[0:90]
        joined[:, 1, :] = extra[96:186]
        for i in range(3):
            for row in range(10):
                out_ref[i, row] = joined[row * 9:row * 9 + 7, i:i + 16, :].astype(BF)


def conv1_end(core, x, e, mine, other, acc, eacc, gain, mask, emask):
    half = pl.BlockSpec((4, D // 2, D), lambda s: (s, 0, 0))
    return pl.pallas_call(
        conv1_end_kernel,
        grid=(3,),
        in_specs=[
            pl.BlockSpec(memory_space=pltpu.SMEM),
            fixed(3, 12, 9, 16, D),
            pl.BlockSpec((4, 192, D), lambda s: (s, 0, 0)),
            half, half, fixed(1120, D), fixed(192, D), fixed(1, D), fixed(1120, 1), fixed(192, 1),
        ],
        out_specs=fixed(3, 10, 7, 16, D),
        out_shape=jax.ShapeDtypeStruct((3, 10, 7, 16, D), BF),
        scratch_shapes=[
            pltpu.VMEM((1120, D), F32),
            pltpu.VMEM((192, D), F32),
            pltpu.VMEM((90, 24, D), F32),
        ],
        compiler_params=pltpu.CompilerParams(vmem_limit_bytes=56 * 2**20),
        name="conv1_end",
    )(core, x, e, mine, other, acc, eacc, gain, mask, emask)


def conv2_kernel(core_ref, x_ref, w_ref, video_ref, *refs):
    halves, (out_ref, acc) = refs[:-2], refs[-2:]
    step = pl.program_id(0)
    windows = [window(x_ref, ROUND2 + 11 * step + n, 8, 5) for n in range(11)]
    taps = [w_ref[n] for n in range(11)]
    total = dot_nt(jnp.concatenate(windows, axis=1), jnp.concatenate(taps, axis=1)).reshape(40, 16, D)

    @pl.when(step == 0)
    def _():
        windows = [window(x_ref, n, 8, 5) for n in range(ROUND2)]
        taps = [joint(core_ref, halves[n][0], halves[ROUND2 + n][0]) for n in range(ROUND2)]
        early = dot_nt(jnp.concatenate(windows, axis=1), jnp.concatenate(taps, axis=1))
        acc[...] = total + early.reshape(40, 16, D)

    @pl.when(step == 1)
    def _():
        acc[...] += total
        for f in range(16):
            out_ref[f] = (video_ref[f].astype(F32) + acc[:, f, :]).astype(BF)


def unit(n):
    return pl.BlockSpec((1, D // 2, D), lambda s: (n, 0, 0))


def conv2(core, x, w, video, mine, other):
    units = [unit(ROUND + n) for n in range(ROUND2)]
    return pl.pallas_call(
        conv2_kernel,
        grid=(2,),
        in_specs=[
            pl.BlockSpec(memory_space=pltpu.SMEM),
            fixed(3, 10, 7, 16, D),
            pl.BlockSpec((11, D, D), lambda s: (s, 0, 0)),
            fixed(16, 40, D),
        ] + units + units,
        out_specs=fixed(16, 40, D),
        out_shape=jax.ShapeDtypeStruct((16, 40, D), BF),
        scratch_shapes=[pltpu.VMEM((40, 16, D), F32)],
        compiler_params=pltpu.CompilerParams(vmem_limit_bytes=56 * 2**20),
        name="conv2",
    )(core, x, w, video, *([mine] * ROUND2), *([other] * ROUND2))


def own_tap(shard1, shard2, ta, ha):
    at = ta * 4 + ha
    taken = jnp.where(
        at < ROUND,
        lax.dynamic_index_in_dim(shard1, jnp.minimum(at, ROUND - 1), 0, keepdims=False),
        lax.dynamic_index_in_dim(shard2, jnp.maximum(at - ROUND, 0), 0, keepdims=False),
    )
    sent = jnp.broadcast_to(taken[None], (16, 24, D))
    return lax.all_to_all(sent, "wa", split_axis=0, concat_axis=0, tiled=True).reshape(2, D // 2, D)


def over_torus(half):
    sent = jnp.broadcast_to(half[None], (16, D // 2, D))
    return lax.all_to_all(sent, ("ta", "ha"), split_axis=0, concat_axis=0, tiled=True)


def swapped(x):
    length = lax.axis_size("wa")
    return lax.ppermute(x, "wa", [(i, i ^ 1) for i in range(length)])


def norm_kernel(block_ref, gain_ref, out_ref):
    out_ref[...] = norm(block_ref[...].astype(F32), gain_ref[...]).astype(BF)


def own_kernel(n_ref, w_ref, asked_ref, top_ref, total_ref, summed_ref):
    own = n_ref[...]
    query = dot_nn(own, w_ref[:, :D]).astype(BF)
    asked = (dot_nt(query, w_ref[:, D:2 * D]) * (D ** -0.5 * 1.4426950408889634)).astype(BF)
    asked_ref[...] = asked
    scores = dot_nt(asked, own)
    top = jnp.max(scores, axis=-1, keepdims=True)
    weights = jnp.exp2(scores - top)
    top_ref[...] = top
    total_ref[...] = jnp.sum(weights, axis=-1, keepdims=True)
    summed_ref[...] = dot_nn(weights.astype(BF), own)


def fold(asked, keys, top, total, summed):
    scores = [dot_nt(asked, k) for k in keys]
    new_top = top
    for s in scores:
        new_top = jnp.maximum(new_top, jnp.max(s, axis=-1, keepdims=True))
    rescale = jnp.exp2(top - new_top)
    total = total * rescale
    summed = summed * rescale
    for s, k in zip(scores, keys):
        weights = jnp.exp2(s - new_top)
        total = total + jnp.sum(weights, axis=-1, keepdims=True)
        summed = summed + dot_nn(weights.astype(BF), k)
    return new_top, total, summed


def mid_kernel(asked_ref, left_ref, right_ref, top_in, total_in, summed_in, top_ref, total_ref, summed_ref):
    top, total, summed = fold(
        asked_ref[...], [left_ref[...], right_ref[...]], top_in[...], total_in[...], summed_in[...]
    )
    top_ref[...] = top
    total_ref[...] = total
    summed_ref[...] = summed


def last_kernel(asked_ref, far0_ref, far1_ref, top_in, total_in, summed_in, w_ref, proj_ref, block_ref, out_ref):
    far = jnp.concatenate([far0_ref[...], far1_ref[...]], axis=0)
    _, total, summed = fold(asked_ref[...], [far], top_in[...], total_in[...], summed_in[...])
    mixed = (summed / total).astype(BF)
    attended = dot_nn(mixed, w_ref[:, 2 * D:]).astype(BF)
    out_ref[...] = (block_ref[...].astype(F32) + dot_nn(attended, proj_ref[...])).astype(BF)


def whole(kernel, outs, name):
    return pl.pallas_call(
        kernel,
        out_shape=outs,
        compiler_params=pltpu.CompilerParams(vmem_limit_bytes=48 * 2**20),
        name=name,
    )


def per_device(video, gain_first, conv_first, gain_second, conv_second, gain_attn, w_qkv, w_proj):
    ta, ha, wa = (lax.axis_index(n) for n in ("ta", "ha", "wa"))
    core = wa % 2
    shard1 = jnp.swapaxes(conv_first, 1, 2)
    kept = lax.all_gather(shard1[ROUND:], "wa", axis=1, tiled=True)
    shard2 = jnp.swapaxes(conv_second, 1, 2)
    filter2 = lax.all_gather(shard2[ROUND2:], "wa", axis=1, tiled=True)
    halves = own_tap(shard1, shard2, ta, ha)
    tall = halo(jnp.concatenate([beside(video[-4:], "ta", 1), video], axis=0), "ha", 1)
    sides = rims(tall, 2)
    halves, *_ = lax.optimization_barrier((halves, *sides))
    mine = over_torus(lax.dynamic_index_in_dim(halves, core, 0, keepdims=False))
    x, round_e, kept_e = prepare(
        turn(beside(sides[0], "wa", 1)), turn(tall), turn(beside(sides[1], "wa", -1)), gain_first.reshape(1, D)
    )

    row = ha * 8 - 1 + jnp.arange(10)
    col = wa * 5 - 1 + jnp.arange(7)
    inside = ((row >= 0) & (row < 8 * lax.axis_size("ha")))[:, None] & ((col >= 0) & (col < 5 * lax.axis_size("wa")))
    inside = inside.astype(F32).reshape(70)
    mask = jnp.repeat(inside, 16).reshape(1120, 1)
    late = jnp.pad(inside.reshape(10, 7), ((0, 0), (0, 2))).reshape(90) * (ta > 0).astype(F32)
    emask = jnp.concatenate([jnp.pad(late, (0, 6))] * 2).reshape(192, 1)

    acc, eacc = conv1_begin(x, kept_e, kept)
    acc, mine = lax.optimization_barrier((acc, mine))
    other = swapped(mine)
    place = core.reshape(1).astype(jnp.int32)
    second = conv1_end(place, x, round_e, mine, other, acc, eacc, gain_second.reshape(1, D), mask, emask)
    block = conv2(place, second, filter2, video.reshape(16, 40, D), mine, other)
    strip = lax.all_to_all(block, "wa", split_axis=0, concat_axis=0, tiled=True).reshape(640, D)

    own = whole(norm_kernel, jax.ShapeDtypeStruct((640, D), BF), "norm")(strip, gain_attn.reshape(1, D))
    right = around(own, "ha", 1)
    left = around(own, "ha", -1)
    stats = [jax.ShapeDtypeStruct((640, 1), F32), jax.ShapeDtypeStruct((640, 1), F32), jax.ShapeDtypeStruct((640, D), F32)]
    asked, *carry = whole(own_kernel, [jax.ShapeDtypeStruct((640, D), BF)] + stats, "own")(own, w_qkv)
    far0 = around(right[:320], "ha", 1)
    far1 = around(left[320:], "ha", -1)
    carry = whole(mid_kernel, stats, "mid")(asked, left, right, *carry)
    out = whole(last_kernel, jax.ShapeDtypeStruct((640, D), BF), "last")(asked, far0, far1, *carry, w_qkv, w_proj, strip)
    out = jnp.transpose(out.reshape(16, 8, 5, D), (1, 0, 2, 3))
    return out.reshape(1, 8, 80, D)


def solution(mesh):
    return jax.shard_map(
        per_device,
        mesh=mesh,
        in_specs=(
            P("ta", "ha", "wa", None),
            P(),
            P(None, None, "wa"),
            P(),
            P(None, None, "wa"),
            P(),
            P(),
            P(),
        ),
        out_specs=P(("ta", "wa"), "ha", None, None),
        check_vma=False,
    )
```

```python
import functools

import jax
import jax.numpy as jnp
from jax import lax
from jax.experimental import pallas as pl
from jax.experimental.pallas import tpu as pltpu
from jax.sharding import PartitionSpec as P

D = 384
ROUND = 11
ROUND2 = 16 - ROUND
BF = jnp.bfloat16
F32 = jnp.float32
NT = (((1,), (1,)), ((), ()))
NN = (((1,), (0,)), ((), ()))


def dot_nt(a, b):
    return lax.dot_general(a, b, NT, preferred_element_type=F32)


def dot_nn(a, b):
    return lax.dot_general(a, b, NN, preferred_element_type=F32)


def norm(wide, gain):
    return wide * lax.rsqrt(jnp.mean(wide * wide, axis=-1, keepdims=True) + 1e-06) * gain


def silu(v):
    return v / (1.0 + jnp.exp(-v))


def beside(x, axis, by):
    length = lax.axis_size(axis)
    pairs = [(i, i + by) for i in range(length) if 0 <= i + by < length]
    return lax.ppermute(x, axis, pairs)


def around(x, axis, by):
    length = lax.axis_size(axis)
    return lax.ppermute(x, axis, [(i, (i + by) % length) for i in range(length)])


def rims(x, dim):
    length = x.shape[dim]
    return lax.slice_in_dim(x, length - 2, length, axis=dim), lax.slice_in_dim(x, 0, 2, axis=dim)


def halo(x, axis, dim):
    late, early = rims(x, dim)
    return jnp.concatenate([beside(late, axis, 1), x, beside(early, axis, -1)], axis=dim)


def fixed(*shape):
    return pl.BlockSpec(shape, lambda s: (0,) * len(shape))


def prepare_kernel(before_ref, tall_ref, after_ref, gain_ref, x_ref, round_ref, kept_ref, turned, flat):
    gain = gain_ref[...]
    for row in range(12):
        cells = slice(row * 9, row * 9 + 9)
        for part, at, count in ((before_ref, 0, 2), (tall_ref, 2, 5), (after_ref, 7, 2)):
            turned[row * 9 + at:row * 9 + at + count, 0:20, :] = silu(
                norm(part[row * count:row * count + count].astype(F32), gain)
            )
        for i in range(3):
            x_ref[i, row] = turned[cells, 2 + i:18 + i, :].astype(BF)
    for f in range(4):
        flat[f, 0:108, :] = turned[:, f, :]
        flat[f, 108:128, :] = jnp.zeros((20, D), F32)
    for tap in range(27):
        i, j, k = tap // 9, tap // 3 % 3, tap % 3
        target, at = (round_ref, tap) if tap < ROUND else (kept_ref, tap - ROUND)
        for f in range(2):
            target[at, f * 96:f * 96 + 96, :] = flat[f + i, 9 * j + k:9 * j + k + 96, :].astype(BF)
    round_ref[ROUND] = jnp.zeros((192, D), BF)


def turn(x):
    return jnp.transpose(x, (1, 2, 0, 3)).reshape(-1, x.shape[0], D)


def prepare(before, tall, after, gain):
    return pl.pallas_call(
        prepare_kernel,
        out_shape=[
            jax.ShapeDtypeStruct((3, 12, 9, 16, D), BF),
            jax.ShapeDtypeStruct((ROUND + 1, 192, D), BF),
            jax.ShapeDtypeStruct((27 - ROUND, 192, D), BF),
        ],
        scratch_shapes=[pltpu.VMEM((108, 24, D), F32), pltpu.VMEM((4, 128, D), F32)],
        compiler_params=pltpu.CompilerParams(vmem_limit_bytes=56 * 2**20),
        name="prepare",
    )(before, tall, after, gain)


def window(x_ref, tap, rows, cols):
    i, j, k = tap // 9, tap // 3 % 3, tap % 3
    return x_ref[i, pl.ds(j, rows), pl.ds(k, cols)].reshape(rows * cols * 16, D)


def conv1_taps(x_ref, e_ref, start, taps):
    windows = [window(x_ref, start + n, 10, 7) for n in range(len(taps))]
    extras = [e_ref[n] for n in range(len(taps))]
    taps = jnp.concatenate(taps, axis=1)
    return dot_nt(jnp.concatenate(windows, axis=1), taps), dot_nt(jnp.concatenate(extras, axis=1), taps)


def conv1_begin_kernel(x_ref, e_ref, w_ref, acc_ref, eacc_ref):
    step = pl.program_id(0)
    total, etotal = conv1_taps(x_ref, e_ref, ROUND + 4 * step, [w_ref[n] for n in range(4)])

    @pl.when(step == 0)
    def _():
        acc_ref[...] = total
        eacc_ref[...] = etotal

    @pl.when(step > 0)
    def _():
        acc_ref[...] += total
        eacc_ref[...] += etotal


def conv1_begin(x, e, w):
    return pl.pallas_call(
        conv1_begin_kernel,
        grid=(4,),
        in_specs=[
            fixed(3, 12, 9, 16, D),
            pl.BlockSpec((4, 192, D), lambda s: (s, 0, 0)),
            pl.BlockSpec((4, D, D), lambda s: (s, 0, 0)),
        ],
        out_specs=[fixed(1120, D), fixed(192, D)],
        out_shape=[jax.ShapeDtypeStruct((1120, D), F32), jax.ShapeDtypeStruct((192, D), F32)],
        compiler_params=pltpu.CompilerParams(vmem_limit_bytes=56 * 2**20),
        name="conv1_begin",
    )(x, e, w)


def joint(core_ref, mine, other):
    first = core_ref[0] == 0
    return jnp.concatenate([jnp.where(first, mine, other), jnp.where(first, other, mine)], axis=0)


def conv1_end_kernel(
    core_ref, x_ref, e_ref, mine_ref, other_ref, acc_in, eacc_in, gain_ref, mask_ref, emask_ref, out_ref, acc, eacc, joined
):
    step = pl.program_id(0)
    taps = [joint(core_ref, mine_ref[n], other_ref[n]) for n in range(4)]
    taps[3] = jnp.where(step == 2, jnp.zeros_like(taps[3]), taps[3])
    total, etotal = conv1_taps(x_ref, e_ref, 4 * step, taps)

    @pl.when(step == 0)
    def _():
        acc[...] = acc_in[...] + total
        eacc[...] = eacc_in[...] + etotal

    @pl.when(step == 1)
    def _():
        acc[...] += total
        eacc[...] += etotal

    @pl.when(step == 2)
    def _():
        gain = gain_ref[...]
        second = (silu(norm(acc[...] + total, gain)) * mask_ref[...]).reshape(70, 16, D)
        for row in range(10):
            joined[row * 9:row * 9 + 7, 2:18, :] = second[row * 7:row * 7 + 7]
        extra = silu(norm(eacc[...] + etotal, gain)) * emask_ref[...]
        joined[:, 0, :] = extra[0:90]
        joined[:, 1, :] = extra[96:186]
        for i in range(3):
            for row in range(10):
                out_ref[i, row] = joined[row * 9:row * 9 + 7, i:i + 16, :].astype(BF)


def conv1_end(core, x, e, mine, other, acc, eacc, gain, mask, emask):
    half = pl.BlockSpec((4, D // 2, D), lambda s: (s, 0, 0))
    return pl.pallas_call(
        conv1_end_kernel,
        grid=(3,),
        in_specs=[
            pl.BlockSpec(memory_space=pltpu.SMEM),
            fixed(3, 12, 9, 16, D),
            pl.BlockSpec((4, 192, D), lambda s: (s, 0, 0)),
            half, half, fixed(1120, D), fixed(192, D), fixed(1, D), fixed(1120, 1), fixed(192, 1),
        ],
        out_specs=fixed(3, 10, 7, 16, D),
        out_shape=jax.ShapeDtypeStruct((3, 10, 7, 16, D), BF),
        scratch_shapes=[
            pltpu.VMEM((1120, D), F32),
            pltpu.VMEM((192, D), F32),
            pltpu.VMEM((90, 24, D), F32),
        ],
        compiler_params=pltpu.CompilerParams(vmem_limit_bytes=56 * 2**20),
        name="conv1_end",
    )(core, x, e, mine, other, acc, eacc, gain, mask, emask)


def conv2_begin_kernel(core_ref, x_ref, *refs):
    halves, acc_ref = refs[:-1], refs[-1]
    windows = [window(x_ref, n, 8, 5) for n in range(ROUND2)]
    taps = [joint(core_ref, halves[n][0], halves[ROUND2 + n][0]) for n in range(ROUND2)]
    early = dot_nt(jnp.concatenate(windows, axis=1), jnp.concatenate(taps, axis=1))
    acc_ref[...] = early.reshape(40, 16, D)


def conv2_kernel(x_ref, w_ref, begun_ref, video_ref, out_ref, acc):
    step = pl.program_id(0)
    windows = [window(x_ref, ROUND2 + 11 * step + n, 8, 5) for n in range(11)]
    taps = [w_ref[n] for n in range(11)]
    total = dot_nt(jnp.concatenate(windows, axis=1), jnp.concatenate(taps, axis=1)).reshape(40, 16, D)

    @pl.when(step == 0)
    def _():
        acc[...] = total + begun_ref[...]

    @pl.when(step == 1)
    def _():
        acc[...] += total
        for f in range(16):
            out_ref[f] = (video_ref[f].astype(F32) + acc[:, f, :]).astype(BF)


def unit(n):
    return pl.BlockSpec((1, D // 2, D), lambda s: (n, 0, 0))


def conv2_begin(core, x, mine, other):
    units = [unit(ROUND + n) for n in range(ROUND2)]
    return pl.pallas_call(
        conv2_begin_kernel,
        grid=(1,),
        in_specs=[pl.BlockSpec(memory_space=pltpu.SMEM), fixed(3, 10, 7, 16, D)] + units + units,
        out_specs=fixed(40, 16, D),
        out_shape=jax.ShapeDtypeStruct((40, 16, D), F32),
        compiler_params=pltpu.CompilerParams(vmem_limit_bytes=56 * 2**20),
        name="conv2_begin",
    )(core, x, *([mine] * ROUND2), *([other] * ROUND2))


def conv2(x, w, begun, video):
    return pl.pallas_call(
        conv2_kernel,
        grid=(2,),
        in_specs=[
            fixed(3, 10, 7, 16, D),
            pl.BlockSpec((11, D, D), lambda s: (s, 0, 0)),
            fixed(40, 16, D),
            fixed(16, 40, D),
        ],
        out_specs=fixed(16, 40, D),
        out_shape=jax.ShapeDtypeStruct((16, 40, D), BF),
        scratch_shapes=[pltpu.VMEM((40, 16, D), F32)],
        compiler_params=pltpu.CompilerParams(vmem_limit_bytes=56 * 2**20),
        name="conv2",
    )(x, w, begun, video)


def own_tap(shard1, shard2, ta, ha):
    at = ta * 4 + ha
    taken = jnp.where(
        at < ROUND,
        lax.dynamic_index_in_dim(shard1, jnp.minimum(at, ROUND - 1), 0, keepdims=False),
        lax.dynamic_index_in_dim(shard2, jnp.maximum(at - ROUND, 0), 0, keepdims=False),
    )
    sent = jnp.broadcast_to(taken[None], (16, 24, D))
    return lax.all_to_all(sent, "wa", split_axis=0, concat_axis=0, tiled=True).reshape(2, D // 2, D)


def over_torus(half):
    sent = jnp.broadcast_to(half[None], (16, D // 2, D))
    return lax.all_to_all(sent, ("ta", "ha"), split_axis=0, concat_axis=0, tiled=True)


def swapped(x):
    length = lax.axis_size("wa")
    return lax.ppermute(x, "wa", [(i, i ^ 1) for i in range(length)])


def norm_kernel(block_ref, gain_ref, out_ref):
    out_ref[...] = norm(block_ref[...].astype(F32), gain_ref[...]).astype(BF)


def own_kernel(n_ref, w_ref, asked_ref, top_ref, total_ref, summed_ref):
    own = n_ref[...]
    query = dot_nn(own, w_ref[:, :D]).astype(BF)
    asked = (dot_nt(query, w_ref[:, D:2 * D]) * (D ** -0.5 * 1.4426950408889634)).astype(BF)
    asked_ref[...] = asked
    scores = dot_nt(asked, own)
    top = jnp.max(scores, axis=-1, keepdims=True)
    weights = jnp.exp2(scores - top)
    top_ref[...] = top
    total_ref[...] = jnp.sum(weights, axis=-1, keepdims=True)
    summed_ref[...] = dot_nn(weights.astype(BF), own)


def fold(asked, keys, top, total, summed):
    scores = [dot_nt(asked, k) for k in keys]
    new_top = top
    for s in scores:
        new_top = jnp.maximum(new_top, jnp.max(s, axis=-1, keepdims=True))
    rescale = jnp.exp2(top - new_top)
    total = total * rescale
    summed = summed * rescale
    for s, k in zip(scores, keys):
        weights = jnp.exp2(s - new_top)
        total = total + jnp.sum(weights, axis=-1, keepdims=True)
        summed = summed + dot_nn(weights.astype(BF), k)
    return new_top, total, summed


def mid_kernel(asked_ref, left_ref, right_ref, top_in, total_in, summed_in, top_ref, total_ref, summed_ref):
    top, total, summed = fold(
        asked_ref[...], [left_ref[...], right_ref[...]], top_in[...], total_in[...], summed_in[...]
    )
    top_ref[...] = top
    total_ref[...] = total
    summed_ref[...] = summed


def last_kernel(asked_ref, far0_ref, far1_ref, top_in, total_in, summed_in, w_ref, proj_ref, block_ref, out_ref):
    far = jnp.concatenate([far0_ref[...], far1_ref[...]], axis=0)
    _, total, summed = fold(asked_ref[...], [far], top_in[...], total_in[...], summed_in[...])
    mixed = (summed / total).astype(BF)
    attended = dot_nn(mixed, w_ref[:, 2 * D:]).astype(BF)
    out_ref[...] = (block_ref[...].astype(F32) + dot_nn(attended, proj_ref[...])).astype(BF)


def whole(kernel, outs, name):
    return pl.pallas_call(
        kernel,
        out_shape=outs,
        compiler_params=pltpu.CompilerParams(vmem_limit_bytes=48 * 2**20),
        name=name,
    )


def per_device(video, gain_first, conv_first, gain_second, conv_second, gain_attn, w_qkv, w_proj):
    ta, ha, wa = (lax.axis_index(n) for n in ("ta", "ha", "wa"))
    core = wa % 2
    shard1 = jnp.swapaxes(conv_first, 1, 2)
    kept = lax.all_gather(shard1[ROUND:], "wa", axis=1, tiled=True)
    shard2 = jnp.swapaxes(conv_second, 1, 2)
    filter2 = lax.all_gather(shard2[ROUND2:], "wa", axis=1, tiled=True)
    halves = own_tap(shard1, shard2, ta, ha)
    tall = halo(jnp.concatenate([beside(video[-4:], "ta", 1), video], axis=0), "ha", 1)
    sides = rims(tall, 2)
    halves, *_ = lax.optimization_barrier((halves, *sides))
    mine = over_torus(lax.dynamic_index_in_dim(halves, core, 0, keepdims=False))
    x, round_e, kept_e = prepare(
        turn(beside(sides[0], "wa", 1)), turn(tall), turn(beside(sides[1], "wa", -1)), gain_first.reshape(1, D)
    )

    row = ha * 8 - 1 + jnp.arange(10)
    col = wa * 5 - 1 + jnp.arange(7)
    inside = ((row >= 0) & (row < 8 * lax.axis_size("ha")))[:, None] & ((col >= 0) & (col < 5 * lax.axis_size("wa")))
    inside = inside.astype(F32).reshape(70)
    mask = jnp.repeat(inside, 16).reshape(1120, 1)
    late = jnp.pad(inside.reshape(10, 7), ((0, 0), (0, 2))).reshape(90) * (ta > 0).astype(F32)
    emask = jnp.concatenate([jnp.pad(late, (0, 6))] * 2).reshape(192, 1)

    acc, eacc = conv1_begin(x, kept_e, kept)
    acc, mine = lax.optimization_barrier((acc, mine))
    other = swapped(mine)
    place = core.reshape(1).astype(jnp.int32)
    second = conv1_end(place, x, round_e, mine, other, acc, eacc, gain_second.reshape(1, D), mask, emask)
    block = conv2(second, filter2, conv2_begin(place, second, mine, other), video.reshape(16, 40, D))
    strip = lax.all_to_all(block, "wa", split_axis=0, concat_axis=0, tiled=True).reshape(640, D)

    own = whole(norm_kernel, jax.ShapeDtypeStruct((640, D), BF), "norm")(strip, gain_attn.reshape(1, D))
    right = around(own, "ha", 1)
    left = around(own, "ha", -1)
    stats = [jax.ShapeDtypeStruct((640, 1), F32), jax.ShapeDtypeStruct((640, 1), F32), jax.ShapeDtypeStruct((640, D), F32)]
    asked, *carry = whole(own_kernel, [jax.ShapeDtypeStruct((640, D), BF)] + stats, "own")(own, w_qkv)
    far0 = around(right[:320], "ha", 1)
    far1 = around(left[320:], "ha", -1)
    carry = whole(mid_kernel, stats, "mid")(asked, left, right, *carry)
    out = whole(last_kernel, jax.ShapeDtypeStruct((640, D), BF), "last")(asked, far0, far1, *carry, w_qkv, w_proj, strip)
    out = jnp.transpose(out.reshape(16, 8, 5, D), (1, 0, 2, 3))
    return out.reshape(1, 8, 80, D)


def solution(mesh):
    return jax.shard_map(
        per_device,
        mesh=mesh,
        in_specs=(
            P("ta", "ha", "wa", None),
            P(),
            P(None, None, "wa"),
            P(),
            P(None, None, "wa"),
            P(),
            P(),
            P(),
        ),
        out_specs=P(("ta", "wa"), "ha", None, None),
        check_vma=False,
    )
```
